32 devices in a mesh: tile: 16 (over z, y, core), layer: 2 (over x).
Axes of the slice: x: 2, y: 2, z: 4, core: 2. Of those that a mesh axis runs over, the one named last changes fastest.
Arguments:
- ensemble: float32 [64, 8, 8192], P(None, 'layer', 'tile'), may hold values from -6 to 6
- diff_x: float32 [8, 8192], P('layer', 'tile'), may hold values from 0.04 to 0.2
- diff_z: float32 [8, 8192], P('layer', 'tile'), may hold values from 0.04 to 0.2
- cour_x: float32 [8, 8192], P('layer', 'tile'), may hold values from -0.4 to 0.4
- cour_z: float32 [8, 8192], P('layer', 'tile'), may hold values from -0.4 to 0.4
- obs_cell: int32 [4, 512], replicated, may hold values from 0 to 65535
- obs_radius: int32 [4, 512], replicated, may hold values from 2048 to 8192
- obs_value: float32 [4, 512], replicated, may hold values from -6 to 6
- obs_var: float32 [4, 512], replicated, may hold values from 0.1 to 1
Outputs:
- posterior: float32 [64, 8, 8192], P(None, 'layer', 'tile')
The draws below stay inside these ranges and needn't reach their ends.
Inputs may be any that keep to these rules, and one draw needn't show every extreme that they name: `obs_cell`: cells are drawn independently over the whole grid; two observations may share a cell.
All inputs are finite; a program needn't handle non-finite values.
Results may differ from the reference program's by a relative error of at most 0.00019.
Values sent between devices are 32-bit elements; how exact they have to be, the bound alone decides.
A program may use at most 64 MiB of HBM per device.

```python
import math
import jax
import jax.numpy as jnp
from jax import lax

MEMBERS = 64
NB = 4
NOBS = 512
NL = 8
NH = 8192


def place_ends(values, rng, low, high):
    longest = values.shape.index(max(values.shape))
    spots = []
    for shift in (0, 1):
        where = [jax.random.randint(jax.random.fold_in(rng, axis), (), 0, length) for axis, length in enumerate(values.shape)]
        where[longest] = (where[longest] + shift) % values.shape[longest]
        spots.append(tuple(where))
    return values.at[spots[0]].set(low).at[spots[1]].set(high)


def level_of(key, extent, pieces, smallest, top_value):
    def one(position, blocks):
        heights = jax.random.uniform(jax.random.fold_in(jax.random.fold_in(key, 6), position), (blocks,), jnp.float32, smallest / len(pieces), top_value / len(pieces))
        return jnp.repeat(jnp.exp(heights), extent[position] // blocks).reshape((-1,) + (1,) * (len(extent) - position - 1))

    loudness = one(*pieces[0])
    for cut in pieces[1:]:
        loudness = loudness * one(*cut)
    return loudness


def normal_values(rng, dims, width, bound, shards=(), kind=jnp.bfloat16):
    entries = jax.random.normal(rng, dims, jnp.float32) * width
    if len(shards) > 0:
        entries = level_of(rng, dims, shards, -0.22, 0.18) * entries
    return jnp.clip(entries, min=-bound, max=bound).astype(kind)


def setup_inputs(seed: int = 0) -> dict:
    keys = jax.random.split(jax.random.key(seed), 10)
    ensemble = normal_values(keys[0], (MEMBERS, NL, NH), 1.0, 6.0, ((1, 2), (2, 16)), jnp.float32)
    diff_x = jnp.clip(jnp.exp(math.log(0.2) - 1.609438 * jax.random.uniform(keys[1], (NL, NH), jnp.float32) ** level_of(keys[1], (NL, NH), ((0, 2), (1, 16)), -0.2, 0.2)), 0.04, 0.2)
    diff_z = jnp.clip(jnp.exp(math.log(0.2) - 1.609438 * jax.random.uniform(keys[2], (NL, NH), jnp.float32) ** level_of(keys[2], (NL, NH), ((0, 2), (1, 16)), -0.2, 0.2)), 0.04, 0.2)
    cour_x = jnp.clip(jax.random.uniform(keys[3], (NL, NH), jnp.float32, -0.4, 0.4) * level_of(keys[3], (NL, NH), ((0, 2), (1, 16)), -0.4, 0.0), -0.4, 0.4)
    cour_z = jnp.clip(jax.random.uniform(keys[4], (NL, NH), jnp.float32, -0.4, 0.4) * level_of(keys[4], (NL, NH), ((0, 2), (1, 16)), -0.4, 0.0), -0.4, 0.4)
    obs_cell = place_ends(jax.random.randint(keys[5], (NB, NOBS), 0, NL * NH), jax.random.fold_in(keys[5], 1), 0, (NL * NH) - 1).astype(jnp.int32)
    obs_radius = place_ends(jax.random.randint(keys[6], (NB, NOBS), NH // 4, NH + 1), jax.random.fold_in(keys[6], 1), NH // 4, NH).astype(jnp.int32)
    obs_value = normal_values(keys[7], (NB, NOBS), 1.0, 6.0, (), jnp.float32)
    obs_var = jnp.clip(jnp.exp(jax.random.uniform(keys[8], (NB, NOBS), jnp.float32, math.log(0.1), math.log(1.0))), 0.1, 1.0)
    return dict(ensemble=ensemble, diff_x=diff_x, diff_z=diff_z, cour_x=cour_x, cour_z=cour_z, obs_cell=obs_cell, obs_radius=obs_radius, obs_value=obs_value, obs_var=obs_var)


def advect(ensemble, diff_x, diff_z, cour_x, cour_z):
    padded = jnp.pad(ensemble, ((0, 0), (1, 1), (1, 1)))
    centre = padded[:, 1:-1, 1:-1]
    upper = padded[:, :-2, 1:-1]
    lower = padded[:, 2:, 1:-1]
    west = padded[:, 1:-1, :-2]
    east = padded[:, 1:-1, 2:]
    return centre + diff_z * (upper - 2.0 * centre + lower) + diff_x * (west - 2.0 * centre + east) - 0.5 * cour_z * (lower - upper) - 0.5 * cour_x * (east - west)

def increments(prior, value, variance):
    members = prior.shape[1]
    ymean = lax.optimization_barrier(jnp.mean(prior, axis=1))
    anomaly = prior - ymean[:, None]
    spread = lax.optimization_barrier(jnp.sum(anomaly * anomaly, axis=1)) / (members - 1) + 1e-06
    shrink = variance / (spread + variance)
    postmean = spread * shrink * (ymean / spread + value / variance)
    delta = (postmean - ymean)[:, None] + (jnp.sqrt(shrink) - 1.0)[:, None] * anomaly
    factor = 1.0 / ((members - 1) * spread)
    return (anomaly, delta, factor)

def taper(positions, centres, radius):
    dist = jnp.abs(positions[None, :] - centres[:, None]).astype(jnp.float32)
    frac = jnp.maximum(1.0 - dist / radius[:, None].astype(jnp.float32), 0.0)
    return frac * frac

def reference(ensemble, diff_x, diff_z, cour_x, cour_z, obs_cell, obs_radius, obs_value, obs_var):
    state = advect(ensemble, diff_x, diff_z, cour_x, cour_z)
    positions = jnp.arange(NH, dtype=jnp.int32)
    for batch in range(NB):
        cells = obs_cell[batch]
        flat = state.reshape(MEMBERS, NL * NH)
        prior = jnp.take(flat, cells, axis=1).T
        anomaly, delta, factor = increments(prior, obs_value[batch], obs_var[batch])
        weight = taper(positions, cells % NH, obs_radius[batch]) * factor[:, None]
        xmean = lax.optimization_barrier(jnp.mean(state, axis=0))
        layered = jnp.transpose(state - xmean[None], (1, 0, 2))

        def one_layer(level):
            cov = jnp.dot(anomaly, level, precision=lax.Precision.HIGHEST)
            return jnp.dot(delta.T, cov * weight, precision=lax.Precision.HIGHEST)
        change = lax.map(one_layer, layered)
        state = state + jnp.transpose(change, (1, 0, 2))
    return state
```

```python
import functools

import jax
import jax.numpy as jnp
from jax import lax
from jax.experimental import pallas as pl
from jax.experimental.pallas import tpu as pltpu
from jax.sharding import PartitionSpec as P

MESH = pl.DeviceIdType.MESH
LANES = 128


def split_cell(cells, total):
    if total & (total - 1) == 0:
        return cells >> (total.bit_length() - 1), cells & (total - 1)
    return cells // total, cells % total


def halves(value):
    high = value.astype(jnp.bfloat16)
    return high, (value - high.astype(jnp.float32)).astype(jnp.bfloat16)


def gather_kernel(
    tiles, layers, ens, diff_x, diff_z, cour_x, cour_z, obs_cell, state, prior,
    cells, edge_w, edge_e, halo_w, halo_e, halo_u, halo_d, part, in_core, in_plane, in_line,
    halo_send, halo_recv, core_sem, plane_send, plane_recv, line_send, line_recv,
):
    members, depth, width = ens.shape
    batches, count = obs_cell.shape
    tile, layer = lax.axis_index("tile"), lax.axis_index("layer")
    core, row, line = tile % 2, (tile // 2) % 2, tile // 4
    plane_n, line_n = layers * 2, tiles // 4
    spot = layer * 2 + row
    pair = (tile + 1 - 2 * core, layer)

    def plane_at(index):
        return (line * 4 + (index % 2) * 2 + core, index // 2)

    def line_at(index):
        return (index * 4 + row * 2 + core, layer)

    greeted = [pair, ((tile + 1) % tiles, layer), ((tile + tiles - 1) % tiles, layer)]
    greeted += [(tile, (layer + 1) % layers), (tile, (layer + layers - 1) % layers)]
    greeted += [plane_at((spot + j) % plane_n) for j in range(1, plane_n)]
    greeted += [line_at((line + j) % line_n) for j in range(1, line_n)]
    barrier = pltpu.get_barrier_semaphore()
    for device in greeted:
        pl.semaphore_signal(barrier, inc=1, device_id=device, device_id_type=MESH)

    lane = lax.broadcasted_iota(jnp.int32, (members, LANES), 1)
    west = jnp.zeros((members, LANES), jnp.float32)
    east = jnp.zeros((members, LANES), jnp.float32)
    for l in range(depth):
        x = ens[:, l, :]
        cells[l] = x
        west = jnp.where(lane == l, x[:, 0:1], west)
        east = jnp.where(lane == l, x[:, width - 1 : width], east)
    edge_w[...] = west
    edge_e[...] = east
    pl.semaphore_wait(barrier, len(greeted))

    def remote(src, dst, send, recv, device):
        return pltpu.make_async_remote_copy(
            src_ref=src, dst_ref=dst, send_sem=send, recv_sem=recv, device_id=device, device_id_type=MESH
        )

    up, down = layer > 0, layer < layers - 1
    before, after = tile > 0, tile < tiles - 1
    moves = (
        (down, up, remote(cells.at[depth - 1], halo_u, halo_send.at[0], halo_recv.at[0], (tile, lax.rem(layer + 1, layers))), halo_u),
        (up, down, remote(cells.at[0], halo_d, halo_send.at[1], halo_recv.at[1], (tile, lax.rem(layer + layers - 1, layers))), halo_d),
        (after, before, remote(edge_e, halo_w, halo_send.at[2], halo_recv.at[2], (lax.rem(tile + 1, tiles), layer)), halo_w),
        (before, after, remote(edge_w, halo_e, halo_send.at[3], halo_recv.at[3], (lax.rem(tile + tiles - 1, tiles), layer)), halo_e),
    )
    for sends, receives, copy, place in moves:
        pl.when(sends)(copy.start)

        @pl.when(jnp.logical_not(receives))
        def _(place=place):
            place[...] = jnp.zeros_like(place)

    for sends, receives, copy, place in moves:
        pl.when(receives)(copy.wait_recv)

    column = lax.broadcasted_iota(jnp.int32, (members, width), 1)
    parts = []
    for l in range(depth):
        x = cells[l]
        upper = halo_u[...] if l == 0 else cells[l - 1]
        lower = halo_d[...] if l == depth - 1 else cells[l + 1]
        left = jnp.where(column == 0, halo_w[:, l : l + 1], pltpu.roll(x, 1, 1))
        right = jnp.where(column == width - 1, halo_e[:, l : l + 1], pltpu.roll(x, width - 1, 1))
        dx, dz = diff_x[l : l + 1, :], diff_z[l : l + 1, :]
        cx, cz = 0.5 * cour_x[l : l + 1, :], 0.5 * cour_z[l : l + 1, :]
        new = (
            x * (1.0 - 2.0 * dz - 2.0 * dx)
            + upper * (dz + cz)
            + lower * (dz - cz)
            + left * (dx + cx)
            + right * (dx - cx)
        )
        state[l] = new
        parts.extend(halves(new))
    stacked = jnp.concatenate(parts, axis=0)

    blocks = count // LANES
    place = lax.broadcasted_iota(jnp.int32, (width, count), 0)
    for b in range(batches):
        rows, cols = split_cell(obs_cell[b : b + 1, :], tiles * width)
        rows, cols = rows - layer * depth, cols - tile * width
        hot = jnp.where(place == cols, 1.0, 0.0).astype(jnp.bfloat16)
        picked = jnp.dot(stacked, hot, preferred_element_type=jnp.float32)
        total = jnp.zeros((members, count), jnp.float32)
        for l in range(depth):
            both = picked[2 * l * members : (2 * l + 1) * members] + picked[(2 * l + 1) * members : (2 * l + 2) * members]
            total = jnp.where(rows == l, both, total)
        for k in range(blocks):
            part[pl.ds((b * blocks + k) * members, members), :] = total[:, k * LANES : (k + 1) * LANES]

    half = part.shape[0] // 2
    mine = pl.multiple_of(core * half, 8)
    other = pl.multiple_of((1 - core) * half, 8)
    copy = remote(part.at[pl.ds(other, half)], in_core, core_sem.at[0], core_sem.at[1], pair)
    copy.start()
    copy.wait_recv()
    core_out = copy
    part[pl.ds(mine, half), :] += in_core[...]

    size = half // plane_n
    base = pl.multiple_of(mine + spot * size, 8)
    plane_out = []
    for j in range(1, plane_n):
        to = (spot + j) % plane_n
        copy = remote(
            part.at[pl.ds(pl.multiple_of(mine + to * size, 8), size)], in_plane.at[j - 1],
            plane_send.at[j - 1], plane_recv.at[j - 1], plane_at(to),
        )
        copy.start()
        plane_out.append(copy)
    total = part[pl.ds(base, size), :]
    for j in range(1, plane_n):
        plane_out[j - 1].wait_recv()
        total = total + in_plane[j - 1]
    part[pl.ds(base, size), :] = total

    scatter = size % (8 * line_n) == 0
    piece = size // line_n if scatter else size
    own = pl.multiple_of(base + line * piece, 8) if scatter else base
    line_out = []
    for j in range(1, line_n):
        to = (line + j) % line_n
        start = pl.multiple_of(base + to * piece, 8) if scatter else base
        copy = remote(part.at[pl.ds(start, piece)], in_line.at[j - 1], line_send.at[j - 1], line_recv.at[j - 1], line_at(to))
        copy.start()
        line_out.append(copy)
    total = part[pl.ds(own, piece), :]
    for j in range(1, line_n):
        line_out[j - 1].wait_recv()
        total = total + in_line[j - 1]
    prior[pl.ds(own, piece), :] = total

    back = []
    if scatter:
        for j in range(1, line_n):
            view = prior.at[pl.ds(own, piece)]
            k = line_n - 1 + j - 1
            copy = remote(view, view, line_send.at[k], line_recv.at[k], line_at((line + j) % line_n))
            copy.start()
            back.append(copy)
        for copy in back:
            copy.wait_recv()
    spread = []
    for j in range(1, plane_n):
        view = prior.at[pl.ds(base, size)]
        k = plane_n - 1 + j - 1
        copy = remote(view, view, plane_send.at[k], plane_recv.at[k], plane_at((spot + j) % plane_n))
        copy.start()
        spread.append(copy)
    for copy in spread:
        copy.wait_recv()
    view = prior.at[pl.ds(mine, half)]
    last = remote(view, view, core_sem.at[2], core_sem.at[3], pair)
    last.start()
    last.wait_recv()
    for copy in [core_out, last] + plane_out + line_out + back + spread:
        copy.wait_send()
    for sends, receives, copy, place in moves:
        pl.when(sends)(copy.wait_send)


def update_kernel(total_cols, width, state, prior, obs_cell, obs_radius, obs_value, obs_var, out, layers_ref, later_ref):
    depth, members, _ = state.shape
    batches, count = obs_cell.shape
    blocks = count // LANES
    first = lax.axis_index("tile") * width
    layers_ref[...] = state[...]
    for b in range(batches):
        for k in range(blocks):
            later_ref[b, :, k * LANES : (k + 1) * LANES] = prior[pl.ds((b * blocks + k) * members, members), :]
    centre = split_cell(obs_cell[...], total_cols)[1].astype(jnp.float32)
    inverse = 1.0 / obs_radius[...].astype(jnp.float32)
    upright = jnp.concatenate([centre, inverse], axis=0).T
    grid = (first + lax.broadcasted_iota(jnp.int32, (1, width), 1)).astype(jnp.float32)

    for b in range(batches):
        y = later_ref[b]
        value, variance = obs_value[b : b + 1, :], obs_var[b : b + 1, :]
        ymean = jnp.sum(y, axis=0, keepdims=True) * (1.0 / members)
        anomaly = y - ymean
        spread = jnp.sum(anomaly * anomaly, axis=0, keepdims=True) / (members - 1) + 1e-06
        shrink = variance / (spread + variance)
        postmean = spread * shrink * (ymean / spread + value / variance)
        delta = (postmean - ymean) + (jnp.sqrt(shrink) - 1.0) * anomaly
        delta = delta * (1.0 / ((members - 1) * spread))
        d_high, d_low = halves(delta)
        d_both = jnp.concatenate([d_high, d_low], axis=0)
        y_high = anomaly.astype(jnp.bfloat16).astype(jnp.float32)
        y_low = anomaly - y_high
        lhs = jnp.concatenate([y_high, y_high, y_low, y_low], axis=0).T.astype(jnp.bfloat16)
        here, scale = upright[:, b : b + 1], upright[:, batches + b : batches + b + 1]

        def taper(positions):
            frac = jnp.maximum(1.0 - jnp.abs(positions - here) * scale, 0.0)
            return frac * frac

        def change(x, weight):
            x_high, x_low = halves(x - jnp.sum(x, axis=0, keepdims=True) * (1.0 / members))
            rhs = jnp.concatenate([x_high, x_low, x_high, x_low], axis=0)
            gain = jnp.dot(lhs, rhs, preferred_element_type=jnp.float32) * weight
            g_high, g_low = halves(gain)
            one = jnp.dot(d_both, g_high, preferred_element_type=jnp.float32)
            two = jnp.dot(d_high, g_low, preferred_element_type=jnp.float32)
            return one[:members] + one[members:] + two

        for c in range(b + 1, batches):
            later_ref[c] += change(later_ref[c], taper(centre[c : c + 1, :]))
        weight = taper(grid)
        for l in range(depth):
            x = layers_ref[l]
            x = x + change(x, weight)
            if b == batches - 1:
                out[:, l, :] = x
            else:
                layers_ref[l] = x


def shards(ensemble, diff_x, diff_z, cour_x, cour_z, obs_cell, obs_radius, obs_value, obs_var):
    members, depth, width = ensemble.shape
    batches, count = obs_cell.shape
    tiles, layers = lax.axis_size("tile"), lax.axis_size("layer")
    rows = batches * count * members // LANES
    plane_n, line_n = layers * 2, tiles // 4
    size = rows // 2 // plane_n
    piece = size // line_n if size % (8 * line_n) == 0 else size
    vmem = pl.BlockSpec(memory_space=pltpu.VMEM)
    f32 = jnp.float32
    state, prior = pl.pallas_call(
        functools.partial(gather_kernel, tiles, layers),
        out_shape=(jax.ShapeDtypeStruct((depth, members, width), f32), jax.ShapeDtypeStruct((rows, LANES), f32)),
        in_specs=[vmem] * 6,
        out_specs=(vmem, vmem),
        scratch_shapes=[
            pltpu.VMEM((depth, members, width), f32),
            pltpu.VMEM((members, LANES), f32),
            pltpu.VMEM((members, LANES), f32),
            pltpu.VMEM((members, LANES), f32),
            pltpu.VMEM((members, LANES), f32),
            pltpu.VMEM((members, width), f32),
            pltpu.VMEM((members, width), f32),
            pltpu.VMEM((rows, LANES), f32),
            pltpu.VMEM((rows // 2, LANES), f32),
            pltpu.VMEM((plane_n - 1, size, LANES), f32),
            pltpu.VMEM((line_n - 1, piece, LANES), f32),
            pltpu.SemaphoreType.DMA((4,)),
            pltpu.SemaphoreType.DMA((4,)),
            pltpu.SemaphoreType.DMA((4,)),
            pltpu.SemaphoreType.DMA((2 * plane_n - 2,)),
            pltpu.SemaphoreType.DMA((2 * plane_n - 2,)),
            pltpu.SemaphoreType.DMA((2 * line_n - 2,)),
            pltpu.SemaphoreType.DMA((2 * line_n - 2,)),
        ],
        compiler_params=pltpu.CompilerParams(collective_id=0, has_side_effects=True, vmem_limit_bytes=40 * 2**20),
        name="gather_prior",
    )(ensemble, diff_x, diff_z, cour_x, cour_z, obs_cell)
    return pl.pallas_call(
        functools.partial(update_kernel, tiles * width, width),
        out_shape=jax.ShapeDtypeStruct((members, depth, width), f32),
        in_specs=[vmem] * 6,
        out_specs=vmem,
        scratch_shapes=[
            pltpu.VMEM((depth, members, width), f32),
            pltpu.VMEM((batches, members, count), f32),
        ],
        compiler_params=pltpu.CompilerParams(vmem_limit_bytes=40 * 2**20),
        name="update",
    )(state, prior, obs_cell, obs_radius, obs_value, obs_var)


def solution(mesh):
    in_specs = (
        P(None, "layer", "tile"),
        P("layer", "tile"),
        P("layer", "tile"),
        P("layer", "tile"),
        P("layer", "tile"),
        P(),
        P(),
        P(),
        P(),
    )
    out_specs = P(None, "layer", "tile")
    return jax.shard_map(shards, mesh=mesh, in_specs=in_specs, out_specs=out_specs, check_vma=False)
```

```python
import functools

import jax
import jax.numpy as jnp
from jax import lax
from jax.experimental import pallas as pl
from jax.experimental.pallas import tpu as pltpu
from jax.sharding import PartitionSpec as P

MESH = pl.DeviceIdType.MESH
LANES = 128


def split_cell(cells, total):
    if total & (total - 1) == 0:
        return cells >> (total.bit_length() - 1), cells & (total - 1)
    return cells // total, cells % total


def halves(value):
    high = value.astype(jnp.bfloat16)
    return high, (value - high.astype(jnp.float32)).astype(jnp.bfloat16)


def gather_kernel(
    tiles, layers, ens_in, dx_in, dz_in, cx_in, cz_in, cell_in, state, prior,
    ens, diff_x, diff_z, cour_x, cour_z, obs_cell, load_sem,
    cells, edge_w, edge_e, halo_w, halo_e, halo_u, halo_d, coef_up, coef_down, coef_u, coef_d,
    part, in_core, in_plane, in_line, halo_send, halo_recv, core_sem, plane_send, plane_recv, line_send, line_recv,
):
    loads = []
    for i, (src, dst) in enumerate(
        ((ens_in, ens), (dz_in, diff_z), (cz_in, cour_z), (dx_in, diff_x), (cx_in, cour_x), (cell_in, obs_cell))
    ):
        copy = pltpu.make_async_copy(src, dst, load_sem.at[i])
        copy.start()
        loads.append(copy)
    members, depth, width = ens.shape
    batches, count = obs_cell.shape
    tile, layer = lax.axis_index("tile"), lax.axis_index("layer")
    core, row, line = tile % 2, (tile // 2) % 2, tile // 4
    plane_n, line_n = layers * 2, tiles // 4
    spot = layer * 2 + row
    pair = (tile + 1 - 2 * core, layer)

    def plane_at(index):
        return (line * 4 + (index % 2) * 2 + core, index // 2)

    def line_at(index):
        return (index * 4 + row * 2 + core, layer)

    greeted = [pair, ((tile + 1) % tiles, layer), ((tile + tiles - 1) % tiles, layer)]
    greeted += [(tile, (layer + 1) % layers), (tile, (layer + layers - 1) % layers)]
    greeted += [plane_at((spot + j) % plane_n) for j in range(1, plane_n)]
    greeted += [line_at((line + j) % line_n) for j in range(1, line_n)]
    barrier = pltpu.get_barrier_semaphore()
    for device in greeted:
        pl.semaphore_signal(barrier, inc=1, device_id=device, device_id_type=MESH)

    for copy in loads:
        copy.wait()
    lane = lax.broadcasted_iota(jnp.int32, (members, LANES), 1)
    west = jnp.zeros((members, LANES), jnp.float32)
    east = jnp.zeros((members, LANES), jnp.float32)
    for l in range(depth):
        x = ens[:, l, :]
        cells[l] = x
        west = jnp.where(lane == l, x[:, 0:1], west)
        east = jnp.where(lane == l, x[:, width - 1 : width], east)
    edge_w[...] = west
    edge_e[...] = east
    tall = coef_up.shape
    coef_up[...] = jnp.broadcast_to(diff_z[0:1, :] + 0.5 * cour_z[0:1, :], tall)
    coef_down[...] = jnp.broadcast_to(diff_z[depth - 1 : depth, :] - 0.5 * cour_z[depth - 1 : depth, :], tall)
    pl.semaphore_wait(barrier, len(greeted))

    def remote(src, dst, send, recv, device):
        return pltpu.make_async_remote_copy(
            src_ref=src, dst_ref=dst, send_sem=send, recv_sem=recv, device_id=device, device_id_type=MESH
        )

    up, down = layer > 0, layer < layers - 1
    before, after = tile > 0, tile < tiles - 1
    above, below = (tile, lax.rem(layer + layers - 1, layers)), (tile, lax.rem(layer + 1, layers))
    ahead, behind = (lax.rem(tile + 1, tiles), layer), (lax.rem(tile + tiles - 1, tiles), layer)

    def move(i, sends, receives, src, dst, device):
        return sends, receives, remote(src, dst, halo_send.at[i], halo_recv.at[i], device), dst

    small = (
        move(0, after, before, edge_e, halo_w, ahead),
        move(1, before, after, edge_w, halo_e, behind),
        move(2, down, up, coef_down, coef_u, below),
        move(3, up, down, coef_up, coef_d, above),
    )
    large = (
        move(4, down, up, cells.at[depth - 1], halo_u, below),
        move(5, up, down, cells.at[0], halo_d, above),
    )
    for sends, receives, copy, place in small:
        pl.when(sends)(copy.start)
    for sends, receives, copy, place in small + large:

        @pl.when(jnp.logical_not(receives))
        def _(place=place):
            place[...] = jnp.zeros_like(place)

    for sends, receives, copy, place in small:
        pl.when(receives)(copy.wait_recv)

    column = lax.broadcasted_iota(jnp.int32, (members, width), 1)
    levels = list(range(depth)) + [-1, depth]
    parts = []
    for l in range(depth):
        x = cells[l]
        left = jnp.where(column == 0, halo_w[:, l : l + 1], pltpu.roll(x, 1, 1))
        right = jnp.where(column == width - 1, halo_e[:, l : l + 1], pltpu.roll(x, width - 1, 1))
        dx, dz = diff_x[l : l + 1, :], diff_z[l : l + 1, :]
        cx, cz = 0.5 * cour_x[l : l + 1, :], 0.5 * cour_z[l : l + 1, :]
        new = x * (1.0 - 2.0 * dz - 2.0 * dx) + left * (dx + cx) + right * (dx - cx)
        if l > 0:
            new = new + cells[l - 1] * (dz + cz)
        if l < depth - 1:
            new = new + cells[l + 1] * (dz - cz)
        state[l] = new
        parts.extend(halves(new))
    parts.extend(halves(cells[0] * coef_u[0:1, :]))
    parts.extend(halves(cells[depth - 1] * coef_d[0:1, :]))
    stacked = jnp.concatenate(parts, axis=0)

    blocks = count // LANES
    extent = blocks * members
    half = extent // 2
    size = half // plane_n
    scatter = size % (8 * line_n) == 0
    piece = size // line_n if scatter else size
    place = lax.broadcasted_iota(jnp.int32, (width, count), 0)

    def start_of(b, *steps):
        total = b * extent
        for index, length in steps:
            total = total + index * length
        return pl.multiple_of(total, 8)

    every = range(batches)
    core_out, plane_out, line_out, line_back, plane_back, core_back = ([[] for _ in every] for _ in range(6))
    for b in every:
        rows, cols = split_cell(obs_cell[b : b + 1, :], tiles * width)
        rows, cols = rows - layer * depth, cols - tile * width
        hot = jnp.where(place == cols, 1.0, 0.0).astype(jnp.bfloat16)
        picked = jnp.dot(stacked, hot, preferred_element_type=jnp.float32)
        total = jnp.zeros((members, count), jnp.float32)
        for i, l in enumerate(levels):
            both = picked[2 * i * members : (2 * i + 1) * members] + picked[(2 * i + 1) * members : (2 * i + 2) * members]
            total = jnp.where(rows == l, both, total)
        for k in range(blocks):
            part[pl.ds((b * blocks + k) * members, members), :] = total[:, k * LANES : (k + 1) * LANES]
        copy = remote(part.at[pl.ds(start_of(b, (1 - core, half)), half)], in_core.at[b], core_sem.at[b, 0], core_sem.at[b, 1], pair)
        copy.start()
        core_out[b].append(copy)

    for b in every:
        core_out[b][0].wait_recv()
        part[pl.ds(start_of(b, (core, half)), half), :] += in_core[b]
        for j in range(1, plane_n):
            to = (spot + j) % plane_n
            copy = remote(
                part.at[pl.ds(start_of(b, (core, half), (to, size)), size)], in_plane.at[b, j - 1],
                plane_send.at[b, j - 1], plane_recv.at[b, j - 1], plane_at(to),
            )
            copy.start()
            plane_out[b].append(copy)
    for b in every:
        base = start_of(b, (core, half), (spot, size))
        total = part[pl.ds(base, size), :]
        for j in range(1, plane_n):
            plane_out[b][j - 1].wait_recv()
            total = total + in_plane[b, j - 1]
        part[pl.ds(base, size), :] = total
        for j in range(1, line_n):
            to = (line + j) % line_n
            start = start_of(b, (core, half), (spot, size), (to, piece)) if scatter else base
            copy = remote(part.at[pl.ds(start, piece)], in_line.at[b, j - 1], line_send.at[b, j - 1], line_recv.at[b, j - 1], line_at(to))
            copy.start()
            line_out[b].append(copy)
    for sends, receives, copy, _ in large:
        pl.when(sends)(copy.start)

    def spread_plane(b):
        view = prior.at[pl.ds(start_of(b, (core, half), (spot, size)), size)]
        for j in range(1, plane_n):
            k = plane_n - 1 + j - 1
            copy = remote(view, view, plane_send.at[b, k], plane_recv.at[b, k], plane_at((spot + j) % plane_n))
            copy.start()
            plane_back[b].append(copy)

    for b in every:
        own = start_of(b, (core, half), (spot, size), (line, piece)) if scatter else start_of(b, (core, half), (spot, size))
        total = part[pl.ds(own, piece), :]
        for j in range(1, line_n):
            line_out[b][j - 1].wait_recv()
            total = total + in_line[b, j - 1]
        prior[pl.ds(own, piece), :] = total
        if scatter:
            view = prior.at[pl.ds(own, piece)]
            for j in range(1, line_n):
                k = line_n - 1 + j - 1
                copy = remote(view, view, line_send.at[b, k], line_recv.at[b, k], line_at((line + j) % line_n))
                copy.start()
                line_back[b].append(copy)
        else:
            spread_plane(b)
    if scatter:
        for b in every:
            for copy in line_back[b]:
                copy.wait_recv()
            spread_plane(b)

    for sends, receives, copy, _ in large:
        pl.when(receives)(copy.wait_recv)
    state[0] += halo_u[...] * (diff_z[0:1, :] + 0.5 * cour_z[0:1, :])
    state[depth - 1] += halo_d[...] * (diff_z[depth - 1 : depth, :] - 0.5 * cour_z[depth - 1 : depth, :])

    for b in every:
        for copy in plane_back[b]:
            copy.wait_recv()
        view = prior.at[pl.ds(start_of(b, (core, half)), half)]
        copy = remote(view, view, core_sem.at[b, 2], core_sem.at[b, 3], pair)
        copy.start()
        core_back[b].append(copy)
    for b in every:
        core_back[b][0].wait_recv()
    for group in (core_out, plane_out, line_out, line_back, plane_back, core_back):
        for copies in group:
            for copy in copies:
                copy.wait_send()
    for sends, receives, copy, _ in small + large:
        pl.when(sends)(copy.wait_send)


def update_kernel(total_cols, width, state, prior, obs_cell, obs_radius, obs_value, obs_var, out, layers_ref, later_ref):
    depth, members, _ = state.shape
    batches, count = obs_cell.shape
    blocks = count // LANES
    first = lax.axis_index("tile") * width
    layers_ref[...] = state[...]
    for b in range(batches):
        for k in range(blocks):
            later_ref[b, :, k * LANES : (k + 1) * LANES] = prior[pl.ds((b * blocks + k) * members, members), :]
    centre = split_cell(obs_cell[...], total_cols)[1].astype(jnp.float32)
    inverse = 1.0 / obs_radius[...].astype(jnp.float32)
    upright = jnp.concatenate([centre, inverse], axis=0).T
    grid = (first + lax.broadcasted_iota(jnp.int32, (1, width), 1)).astype(jnp.float32)

    for b in range(batches):
        y = later_ref[b]
        value, variance = obs_value[b : b + 1, :], obs_var[b : b + 1, :]
        ymean = jnp.sum(y, axis=0, keepdims=True) * (1.0 / members)
        anomaly = y - ymean
        spread = jnp.sum(anomaly * anomaly, axis=0, keepdims=True) / (members - 1) + 1e-06
        shrink = variance / (spread + variance)
        postmean = spread * shrink * (ymean / spread + value / variance)
        delta = (postmean - ymean) + (jnp.sqrt(shrink) - 1.0) * anomaly
        delta = delta * (1.0 / ((members - 1) * spread))
        d_high, d_low = halves(delta)
        d_both = jnp.concatenate([d_high, d_low], axis=0)
        y_high = anomaly.astype(jnp.bfloat16).astype(jnp.float32)
        y_low = anomaly - y_high
        lhs = jnp.concatenate([y_high, y_high, y_low, y_low], axis=0).T.astype(jnp.bfloat16)
        here, scale = upright[:, b : b + 1], upright[:, batches + b : batches + b + 1]

        def taper(positions):
            frac = jnp.maximum(1.0 - jnp.abs(positions - here) * scale, 0.0)
            return frac * frac

        def change(x, weight):
            x_high, x_low = halves(x - jnp.sum(x, axis=0, keepdims=True) * (1.0 / members))
            rhs = jnp.concatenate([x_high, x_low, x_high, x_low], axis=0)
            gain = jnp.dot(lhs, rhs, preferred_element_type=jnp.float32) * weight
            g_high, g_low = halves(gain)
            one = jnp.dot(d_both, g_high, preferred_element_type=jnp.float32)
            two = jnp.dot(d_high, g_low, preferred_element_type=jnp.float32)
            return one[:members] + one[members:] + two

        for c in range(b + 1, batches):
            later_ref[c] += change(later_ref[c], taper(centre[c : c + 1, :]))
        weight = taper(grid)
        for l in range(depth):
            x = layers_ref[l]
            x = x + change(x, weight)
            if b == batches - 1:
                out[:, l, :] = x
            else:
                layers_ref[l] = x


def shards(ensemble, diff_x, diff_z, cour_x, cour_z, obs_cell, obs_radius, obs_value, obs_var):
    members, depth, width = ensemble.shape
    batches, count = obs_cell.shape
    tiles, layers = lax.axis_size("tile"), lax.axis_size("layer")
    rows = batches * count * members // LANES
    plane_n, line_n = layers * 2, tiles // 4
    half = rows // batches // 2
    size = half // plane_n
    piece = size // line_n if size % (8 * line_n) == 0 else size
    vmem = pl.BlockSpec(memory_space=pltpu.VMEM)
    f32 = jnp.float32
    dma = pltpu.SemaphoreType.DMA
    state, prior = pl.pallas_call(
        functools.partial(gather_kernel, tiles, layers),
        out_shape=(jax.ShapeDtypeStruct((depth, members, width), f32), jax.ShapeDtypeStruct((rows, LANES), f32)),
        in_specs=[pl.BlockSpec(memory_space=pltpu.HBM)] * 6,
        out_specs=(vmem, vmem),
        scratch_shapes=[
            pltpu.VMEM((members, depth, width), f32),
            *[pltpu.VMEM((depth, width), f32)] * 4,
            pltpu.VMEM((batches, count), jnp.int32),
            dma((6,)),
            pltpu.VMEM((depth, members, width), f32),
            *[pltpu.VMEM((members, LANES), f32)] * 4,
            *[pltpu.VMEM((members, width), f32)] * 2,
            *[pltpu.VMEM((8, width), f32)] * 4,
            pltpu.VMEM((rows, LANES), f32),
            pltpu.VMEM((batches, half, LANES), f32),
            pltpu.VMEM((batches, plane_n - 1, size, LANES), f32),
            pltpu.VMEM((batches, line_n - 1, piece, LANES), f32),
            dma((6,)),
            dma((6,)),
            dma((batches, 4)),
            dma((batches, 2 * plane_n - 2)),
            dma((batches, 2 * plane_n - 2)),
            dma((batches, 2 * line_n - 2)),
            dma((batches, 2 * line_n - 2)),
        ],
        compiler_params=pltpu.CompilerParams(collective_id=0, has_side_effects=True, vmem_limit_bytes=40 * 2**20),
        name="gather_prior",
    )(ensemble, diff_x, diff_z, cour_x, cour_z, obs_cell)
    return pl.pallas_call(
        functools.partial(update_kernel, tiles * width, width),
        out_shape=jax.ShapeDtypeStruct((members, depth, width), f32),
        in_specs=[vmem] * 6,
        out_specs=vmem,
        scratch_shapes=[
            pltpu.VMEM((depth, members, width), f32),
            pltpu.VMEM((batches, members, count), f32),
        ],
        compiler_params=pltpu.CompilerParams(vmem_limit_bytes=40 * 2**20),
        name="update",
    )(state, prior, obs_cell, obs_radius, obs_value, obs_var)


def solution(mesh):
    in_specs = (
        P(None, "layer", "tile"),
        P("layer", "tile"),
        P("layer", "tile"),
        P("layer", "tile"),
        P("layer", "tile"),
        P(),
        P(),
        P(),
        P(),
    )
    out_specs = P(None, "layer", "tile")
    return jax.shard_map(shards, mesh=mesh, in_specs=in_specs, out_specs=out_specs, check_vma=False)
```

```python
import functools

import jax
import jax.numpy as jnp
from jax import lax
from jax.experimental import pallas as pl
from jax.experimental.pallas import tpu as pltpu
from jax.sharding import PartitionSpec as P

MESH = pl.DeviceIdType.MESH
LANES = 128


def split_cell(cells, total):
    if total & (total - 1) == 0:
        return cells >> (total.bit_length() - 1), cells & (total - 1)
    return cells // total, cells % total


def halves(value):
    high = value.astype(jnp.bfloat16)
    return high, (value - high.astype(jnp.float32)).astype(jnp.bfloat16)


def gather_kernel(
    tiles, layers, ens_in, dx_in, dz_in, cx_in, cz_in, cell_in, state_out, prior,
    state, state_sem, ens, diff_x, diff_z, cour_x, cour_z, obs_cell, load_sem,
    cells, edge_w, edge_e, halo_w, halo_e, halo_u, halo_d, coef_up, coef_down, coef_u, coef_d,
    part, in_core, in_plane, in_line, halo_send, halo_recv, core_sem, plane_send, plane_recv, line_send, line_recv,
):
    loads = []
    for i, (src, dst) in enumerate(
        ((ens_in, ens), (dz_in, diff_z), (cz_in, cour_z), (dx_in, diff_x), (cx_in, cour_x), (cell_in, obs_cell))
    ):
        copy = pltpu.make_async_copy(src, dst, load_sem.at[i])
        copy.start()
        loads.append(copy)
    members, depth, width = ens.shape
    batches, count = obs_cell.shape
    tile, layer = lax.axis_index("tile"), lax.axis_index("layer")
    core, row, line = tile % 2, (tile // 2) % 2, tile // 4
    plane_n, line_n = layers * 2, tiles // 4
    spot = layer * 2 + row
    pair = (tile + 1 - 2 * core, layer)

    def plane_at(index):
        return (line * 4 + (index % 2) * 2 + core, index // 2)

    def line_at(index):
        return (index * 4 + row * 2 + core, layer)

    greeted = [pair, ((tile + 1) % tiles, layer), ((tile + tiles - 1) % tiles, layer)]
    greeted += [(tile, (layer + 1) % layers), (tile, (layer + layers - 1) % layers)]
    greeted += [plane_at((spot + j) % plane_n) for j in range(1, plane_n)]
    greeted += [line_at((line + j) % line_n) for j in range(1, line_n)]
    barrier = pltpu.get_barrier_semaphore()
    for device in greeted:
        pl.semaphore_signal(barrier, inc=1, device_id=device, device_id_type=MESH)

    for copy in loads:
        copy.wait()
    lane = lax.broadcasted_iota(jnp.int32, (members, LANES), 1)
    west = jnp.zeros((members, LANES), jnp.float32)
    east = jnp.zeros((members, LANES), jnp.float32)
    for l in range(depth):
        x = ens[:, l, :]
        cells[l] = x
        west = jnp.where(lane == l, x[:, 0:1], west)
        east = jnp.where(lane == l, x[:, width - 1 : width], east)
    edge_w[...] = west
    edge_e[...] = east
    tall = coef_up.shape
    coef_up[...] = jnp.broadcast_to(diff_z[0:1, :] + 0.5 * cour_z[0:1, :], tall)
    coef_down[...] = jnp.broadcast_to(diff_z[depth - 1 : depth, :] - 0.5 * cour_z[depth - 1 : depth, :], tall)
    pl.semaphore_wait(barrier, len(greeted))

    def remote(src, dst, send, recv, device):
        return pltpu.make_async_remote_copy(
            src_ref=src, dst_ref=dst, send_sem=send, recv_sem=recv, device_id=device, device_id_type=MESH
        )

    up, down = layer > 0, layer < layers - 1
    before, after = tile > 0, tile < tiles - 1
    above, below = (tile, lax.rem(layer + layers - 1, layers)), (tile, lax.rem(layer + 1, layers))
    ahead, behind = (lax.rem(tile + 1, tiles), layer), (lax.rem(tile + tiles - 1, tiles), layer)

    def move(i, sends, receives, src, dst, device):
        return sends, receives, remote(src, dst, halo_send.at[i], halo_recv.at[i], device), dst

    small = (
        move(0, after, before, edge_e, halo_w, ahead),
        move(1, before, after, edge_w, halo_e, behind),
        move(2, down, up, coef_down, coef_u, below),
        move(3, up, down, coef_up, coef_d, above),
    )
    large = (
        move(4, down, up, cells.at[depth - 1], halo_u, below),
        move(5, up, down, cells.at[0], halo_d, above),
    )
    for sends, receives, copy, place in small:
        pl.when(sends)(copy.start)
    for sends, receives, copy, place in small + large:

        @pl.when(jnp.logical_not(receives))
        def _(place=place):
            place[...] = jnp.zeros_like(place)

    for sends, receives, copy, place in small:
        pl.when(receives)(copy.wait_recv)

    column = lax.broadcasted_iota(jnp.int32, (members, width), 1)
    levels = list(range(depth)) + [-1, depth]
    parts = []
    for l in range(depth):
        x = cells[l]
        left = jnp.where(column == 0, halo_w[:, l : l + 1], pltpu.roll(x, 1, 1))
        right = jnp.where(column == width - 1, halo_e[:, l : l + 1], pltpu.roll(x, width - 1, 1))
        dx, dz = diff_x[l : l + 1, :], diff_z[l : l + 1, :]
        cx, cz = 0.5 * cour_x[l : l + 1, :], 0.5 * cour_z[l : l + 1, :]
        new = x * (1.0 - 2.0 * dz - 2.0 * dx) + left * (dx + cx) + right * (dx - cx)
        if l > 0:
            new = new + cells[l - 1] * (dz + cz)
        if l < depth - 1:
            new = new + cells[l + 1] * (dz - cz)
        state[l] = new
        parts.extend(halves(new))
    parts.extend(halves(cells[0] * coef_u[0:1, :]))
    parts.extend(halves(cells[depth - 1] * coef_d[0:1, :]))
    stacked = jnp.concatenate(parts, axis=0)

    blocks = count // LANES
    extent = blocks * members
    half = extent // 2
    size = half // plane_n
    scatter = size % (8 * line_n) == 0
    piece = size // line_n if scatter else size
    place = lax.broadcasted_iota(jnp.int32, (width, count), 0)

    def start_of(b, *steps):
        total = b * extent
        for index, length in steps:
            total = total + index * length
        return pl.multiple_of(total, 8)

    every = range(batches)
    core_out, plane_out, line_out, line_back, plane_back, core_back = ([[] for _ in every] for _ in range(6))
    for b in every:
        rows, cols = split_cell(obs_cell[b : b + 1, :], tiles * width)
        rows, cols = rows - layer * depth, cols - tile * width
        hot = jnp.where(place == cols, 1.0, 0.0).astype(jnp.bfloat16)
        picked = jnp.dot(stacked, hot, preferred_element_type=jnp.float32)
        total = jnp.zeros((members, count), jnp.float32)
        for i, l in enumerate(levels):
            both = picked[2 * i * members : (2 * i + 1) * members] + picked[(2 * i + 1) * members : (2 * i + 2) * members]
            total = jnp.where(rows == l, both, total)
        for k in range(blocks):
            part[pl.ds((b * blocks + k) * members, members), :] = total[:, k * LANES : (k + 1) * LANES]
        copy = remote(part.at[pl.ds(start_of(b, (1 - core, half)), half)], in_core.at[b], core_sem.at[b, 0], core_sem.at[b, 1], pair)
        copy.start()
        core_out[b].append(copy)

    for b in every:
        core_out[b][0].wait_recv()
        part[pl.ds(start_of(b, (core, half)), half), :] += in_core[b]
        for j in range(1, plane_n):
            to = (spot + j) % plane_n
            copy = remote(
                part.at[pl.ds(start_of(b, (core, half), (to, size)), size)], in_plane.at[b, j - 1],
                plane_send.at[b, j - 1], plane_recv.at[b, j - 1], plane_at(to),
            )
            copy.start()
            plane_out[b].append(copy)
    for b in every:
        base = start_of(b, (core, half), (spot, size))
        total = part[pl.ds(base, size), :]
        for j in range(1, plane_n):
            plane_out[b][j - 1].wait_recv()
            total = total + in_plane[b, j - 1]
        part[pl.ds(base, size), :] = total
        for j in range(1, line_n):
            to = (line + j) % line_n
            start = start_of(b, (core, half), (spot, size), (to, piece)) if scatter else base
            copy = remote(part.at[pl.ds(start, piece)], in_line.at[b, j - 1], line_send.at[b, j - 1], line_recv.at[b, j - 1], line_at(to))
            copy.start()
            line_out[b].append(copy)
    for sends, receives, copy, _ in large:
        pl.when(sends)(copy.start)

    def spread_plane(b):
        view = prior.at[pl.ds(start_of(b, (core, half), (spot, size)), size)]
        for j in range(1, plane_n):
            k = plane_n - 1 + j - 1
            copy = remote(view, view, plane_send.at[b, k], plane_recv.at[b, k], plane_at((spot + j) % plane_n))
            copy.start()
            plane_back[b].append(copy)

    for b in every:
        own = start_of(b, (core, half), (spot, size), (line, piece)) if scatter else start_of(b, (core, half), (spot, size))
        total = part[pl.ds(own, piece), :]
        for j in range(1, line_n):
            line_out[b][j - 1].wait_recv()
            total = total + in_line[b, j - 1]
        prior[pl.ds(own, piece), :] = total
        if scatter:
            view = prior.at[pl.ds(own, piece)]
            for j in range(1, line_n):
                k = line_n - 1 + j - 1
                copy = remote(view, view, line_send.at[b, k], line_recv.at[b, k], line_at((line + j) % line_n))
                copy.start()
                line_back[b].append(copy)
        else:
            spread_plane(b)
    if scatter:
        for b in every:
            for copy in line_back[b]:
                copy.wait_recv()
            spread_plane(b)

    for sends, receives, copy, _ in large:
        pl.when(receives)(copy.wait_recv)
    state[0] += halo_u[...] * (diff_z[0:1, :] + 0.5 * cour_z[0:1, :])
    state[depth - 1] += halo_d[...] * (diff_z[depth - 1 : depth, :] - 0.5 * cour_z[depth - 1 : depth, :])
    keep = pltpu.make_async_copy(state, state_out, state_sem)
    keep.start()

    for b in every:
        for copy in plane_back[b]:
            copy.wait_recv()
        view = prior.at[pl.ds(start_of(b, (core, half)), half)]
        copy = remote(view, view, core_sem.at[b, 2], core_sem.at[b, 3], pair)
        copy.start()
        core_back[b].append(copy)
    for b in every:
        core_back[b][0].wait_recv()
    for group in (core_out, plane_out, line_out, line_back, plane_back, core_back):
        for copies in group:
            for copy in copies:
                copy.wait_send()
    for sends, receives, copy, _ in small + large:
        pl.when(sends)(copy.wait_send)
    keep.wait()


def update_kernel(
    total_cols, width, state_in, prior_in, cell_in, radius_in, value_in, var_in, out,
    layers_ref, later_ref, prior, obs_cell, obs_radius, obs_value, obs_var, load_sem,
):
    loads = []
    for i, (src, dst) in enumerate(
        (
            (cell_in, obs_cell), (radius_in, obs_radius), (value_in, obs_value), (var_in, obs_var),
            (prior_in, prior), (state_in, layers_ref),
        )
    ):
        copy = pltpu.make_async_copy(src, dst, load_sem.at[i])
        copy.start()
        loads.append(copy)
    depth, members, _ = layers_ref.shape
    batches, count = obs_cell.shape
    blocks = count // LANES
    first = lax.axis_index("tile") * width
    for copy in loads[:-1]:
        copy.wait()
    for b in range(batches):
        for k in range(blocks):
            later_ref[b, :, k * LANES : (k + 1) * LANES] = prior[pl.ds((b * blocks + k) * members, members), :]
    centre = split_cell(obs_cell[...], total_cols)[1].astype(jnp.float32)
    inverse = 1.0 / obs_radius[...].astype(jnp.float32)
    upright = jnp.concatenate([centre, inverse], axis=0).T
    grid = (first + lax.broadcasted_iota(jnp.int32, (1, width), 1)).astype(jnp.float32)

    for b in range(batches):
        y = later_ref[b]
        value, variance = obs_value[b : b + 1, :], obs_var[b : b + 1, :]
        ymean = jnp.sum(y, axis=0, keepdims=True) * (1.0 / members)
        anomaly = y - ymean
        spread = jnp.sum(anomaly * anomaly, axis=0, keepdims=True) / (members - 1) + 1e-06
        shrink = variance / (spread + variance)
        postmean = spread * shrink * (ymean / spread + value / variance)
        delta = (postmean - ymean) + (jnp.sqrt(shrink) - 1.0) * anomaly
        delta = delta * (1.0 / ((members - 1) * spread))
        d_high, d_low = halves(delta)
        d_both = jnp.concatenate([d_high, d_low], axis=0)
        y_high = anomaly.astype(jnp.bfloat16).astype(jnp.float32)
        y_low = anomaly - y_high
        lhs = jnp.concatenate([y_high, y_high, y_low, y_low], axis=0).T.astype(jnp.bfloat16)
        here, scale = upright[:, b : b + 1], upright[:, batches + b : batches + b + 1]

        def taper(positions):
            frac = jnp.maximum(1.0 - jnp.abs(positions - here) * scale, 0.0)
            return frac * frac

        def change(x, weight):
            x_high, x_low = halves(x - jnp.sum(x, axis=0, keepdims=True) * (1.0 / members))
            rhs = jnp.concatenate([x_high, x_low, x_high, x_low], axis=0)
            gain = jnp.dot(lhs, rhs, preferred_element_type=jnp.float32) * weight
            g_high, g_low = halves(gain)
            one = jnp.dot(d_both, g_high, preferred_element_type=jnp.float32)
            two = jnp.dot(d_high, g_low, preferred_element_type=jnp.float32)
            return one[:members] + one[members:] + two

        for c in range(b + 1, batches):
            later_ref[c] += change(later_ref[c], taper(centre[c : c + 1, :]))
        weight = taper(grid)
        if b == 0:
            loads[-1].wait()
        for l in range(depth):
            x = layers_ref[l]
            x = x + change(x, weight)
            if b == batches - 1:
                out[:, l, :] = x
            else:
                layers_ref[l] = x


def shards(ensemble, diff_x, diff_z, cour_x, cour_z, obs_cell, obs_radius, obs_value, obs_var):
    members, depth, width = ensemble.shape
    batches, count = obs_cell.shape
    tiles, layers = lax.axis_size("tile"), lax.axis_size("layer")
    rows = batches * count * members // LANES
    plane_n, line_n = layers * 2, tiles // 4
    half = rows // batches // 2
    size = half // plane_n
    piece = size // line_n if size % (8 * line_n) == 0 else size
    vmem = pl.BlockSpec(memory_space=pltpu.VMEM)
    hbm = pl.BlockSpec(memory_space=pltpu.HBM)
    f32 = jnp.float32
    dma = pltpu.SemaphoreType.DMA
    state, prior = pl.pallas_call(
        functools.partial(gather_kernel, tiles, layers),
        out_shape=(jax.ShapeDtypeStruct((depth, members, width), f32), jax.ShapeDtypeStruct((rows, LANES), f32)),
        in_specs=[hbm] * 6,
        out_specs=(hbm, vmem),
        scratch_shapes=[
            pltpu.VMEM((depth, members, width), f32),
            dma,
            pltpu.VMEM((members, depth, width), f32),
            *[pltpu.VMEM((depth, width), f32)] * 4,
            pltpu.VMEM((batches, count), jnp.int32),
            dma((6,)),
            pltpu.VMEM((depth, members, width), f32),
            *[pltpu.VMEM((members, LANES), f32)] * 4,
            *[pltpu.VMEM((members, width), f32)] * 2,
            *[pltpu.VMEM((8, width), f32)] * 4,
            pltpu.VMEM((rows, LANES), f32),
            pltpu.VMEM((batches, half, LANES), f32),
            pltpu.VMEM((batches, plane_n - 1, size, LANES), f32),
            pltpu.VMEM((batches, line_n - 1, piece, LANES), f32),
            dma((6,)),
            dma((6,)),
            dma((batches, 4)),
            dma((batches, 2 * plane_n - 2)),
            dma((batches, 2 * plane_n - 2)),
            dma((batches, 2 * line_n - 2)),
            dma((batches, 2 * line_n - 2)),
        ],
        compiler_params=pltpu.CompilerParams(collective_id=0, has_side_effects=True, vmem_limit_bytes=63 * 2**20),
        name="gather_prior",
    )(ensemble, diff_x, diff_z, cour_x, cour_z, obs_cell)
    return pl.pallas_call(
        functools.partial(update_kernel, tiles * width, width),
        out_shape=jax.ShapeDtypeStruct((members, depth, width), f32),
        in_specs=[hbm] * 6,
        out_specs=vmem,
        scratch_shapes=[
            pltpu.VMEM((depth, members, width), f32),
            pltpu.VMEM((batches, members, count), f32),
            pltpu.VMEM((rows, LANES), f32),
            *[pltpu.VMEM((batches, count), jnp.int32)] * 2,
            *[pltpu.VMEM((batches, count), f32)] * 2,
            dma((6,)),
        ],
        compiler_params=pltpu.CompilerParams(vmem_limit_bytes=63 * 2**20),
        name="update",
    )(state, prior, obs_cell, obs_radius, obs_value, obs_var)


def solution(mesh):
    in_specs = (
        P(None, "layer", "tile"),
        P("layer", "tile"),
        P("layer", "tile"),
        P("layer", "tile"),
        P("layer", "tile"),
        P(),
        P(),
        P(),
        P(),
    )
    out_specs = P(None, "layer", "tile")
    return jax.shard_map(shards, mesh=mesh, in_specs=in_specs, out_specs=out_specs, check_vma=False)
```
